256 devices in a mesh: row: 2 (over x_lo), col: 128 (over x_hi, y, z, core).
Axes of the slice: x: 4 (x_hi: 2, x_lo: 2; x = x_hi * 2 + x_lo), y: 4, z: 8, core: 2. Of those that a mesh axis runs over, the one named last changes fastest.
Arguments:
- matrix: float32 [64, 2, 128, 1, 128, 128], P(None, 'row', None, None, 'col'), may hold values from -0.25 to 1.5, as said below
Outputs:
- factored: float32 [64, 2, 128, 1, 128, 128], P(None, 'row', None, None, 'col')
The draws below stay inside these ranges and needn't reach their ends.
Inputs may be any that keep to these rules, and one draw needn't show every extreme that they name: matrix read as A is symmetric and positive definite, its eigenvalues between 0.4 and 8.
All inputs are finite; a program needn't handle non-finite values.
Results may differ from the reference program's by a relative error of at most 0.0001.
Values sent between devices are 32-bit elements; how exact they have to be, the bound alone decides.
A program may use at most 64 MiB of HBM per device.

```python
import math
import jax
import jax.numpy as jnp
from jax import lax

NB = 128
COLB = 1
STEPS = 1
ORDER = 16384
ROWB = 64


def draw_matrix(key, part):
    key = jax.random.fold_in(key, 7)
    noise_key, gain_key, shared_key = jax.random.split(key, 3)
    sample = jnp.clip(jax.random.normal(noise_key, (ORDER, ORDER), jnp.float32), -6.0, 6.0)
    gains = jnp.exp(jax.random.uniform(gain_key, (ORDER,), jnp.float32, math.log(0.8), math.log(1.2)))
    shared = jax.random.uniform(shared_key, (ORDER,), jnp.float32, 0.5, 1.0)
    noise = (sample + sample.T) * (0.25 * math.sqrt(0.5) / math.sqrt(ORDER))
    place = jnp.arange(ORDER, dtype=jnp.float32)
    spacing = (place[:, None] - place[None, :]) * 0.125
    kernel = 0.18 * gains[:, None] * gains[None, :] * jnp.exp(-0.5 * spacing * spacing)
    common = shared[:, None] * shared[None, :] * (1.0 / ORDER)
    full = kernel + common + noise + jnp.eye(ORDER, dtype=jnp.float32)
    row_owners = ORDER // (ROWB * NB)
    col_owners = ORDER // (COLB * NB)
    return full.reshape(ROWB, row_owners, NB, COLB, col_owners, NB)


def setup_inputs(seed: int = 0) -> dict:
    streams_of = jax.random.split(jax.random.key(seed), 2)
    matrix = draw_matrix(jax.random.fold_in(streams_of[1], 71), 0)
    return dict(matrix=matrix)


def reference(matrix):
    shape = matrix.shape
    full = matrix.reshape(ORDER, ORDER)
    row_block = jnp.arange(ORDER) // NB
    for step in range(STEPS):
        start = step * NB
        finish = start + NB
        factor = jnp.linalg.cholesky(full[start:finish, start:finish])
        column = full[:, start:finish]
        solved = jax.scipy.linalg.solve_triangular(factor, column.T, lower=True).T
        tail_rows = solved[finish:]
        full = full.at[finish:, finish:].add(-jnp.dot(tail_rows, tail_rows.T, precision=lax.Precision.HIGHEST))
        diag_rows = jnp.tile(factor, (ORDER // NB, 1))
        new_column = jnp.where(row_block[:, None] > step, solved, jnp.where(row_block[:, None] == step, diag_rows, 0.0))
        full = full.at[:, start:finish].set(new_column)
    return full.reshape(shape)
```

```python
import functools

import jax
import jax.numpy as jnp
from jax import lax
from jax.experimental import pallas as pl
from jax.experimental.pallas import tpu as pltpu
from jax.sharding import PartitionSpec as P

F32 = jnp.float32
BF16 = jnp.bfloat16
NB = 128
HALF = NB // 2
BLOCKS = 64
NX, NY, NZ = 2, 4, 8
NXY = NX * NY
PIVOTS = 16


def split3(x):
    first = x.astype(BF16)
    rest = x - first.astype(F32)
    second = rest.astype(BF16)
    return first, second, (rest - second.astype(F32)).astype(BF16)


def outer(u, t):
    u1, u2, u3 = split3(u)
    t1, t2, t3 = split3(t)
    left = jnp.concatenate([u1, u1, u2, u2, u1, u3], 0)
    right = jnp.concatenate([t1, t2, t1, t2, t3, t1], 0)
    return lax.dot_general(left, right, (((0,), (0,)), ((), ())), preferred_element_type=F32)


def sweep_block(m_ref, ft_ref, block):
    b = PIVOTS
    groups = b // 8
    o = block * b
    sub = lax.broadcasted_iota(jnp.int32, (8, NB), 0)
    lane = lax.broadcasted_iota(jnp.int32, (8, NB), 1)
    rows = [m_ref[o + 8 * t : o + 8 * t + 8, :] for t in range(groups)]
    work = list(rows)
    cols = [[jnp.broadcast_to(rows[t][:, o + j : o + j + 1], (8, NB)) for t in range(groups)] for j in range(b)]
    factor = [None] * groups
    for j in range(b):
        tj, sj = divmod(j, 8)
        pivot = cols[j][tj][sj : sj + 1, :]
        inverse = 1.0 / pivot
        line = work[tj][sj : sj + 1, :] * lax.rsqrt(pivot)
        factor[tj] = jnp.broadcast_to(line, (8, NB)) if sj == 0 else jnp.where(sub == sj, line, factor[tj])
        work = [
            jnp.where(lane == o + j, jnp.where(sub == sj, 1.0, 0.0) if t == tj else 0.0, work[t])
            for t in range(groups)
        ]
        by = list(cols[j])
        by[tj] = jnp.where(sub == sj, cols[j][tj] - 1.0, cols[j][tj])
        scaled = work[tj][sj : sj + 1, :] * inverse
        work = [work[t] - by[t] * scaled for t in range(groups)]
        for m in range(j + 1, b):
            one = cols[m][tj][sj : sj + 1, :] * inverse
            cols[m] = [cols[m][t] - by[t] * one for t in range(groups)]
    inside = (lane >= o) & (lane < o + b)
    eye = [jnp.where(lane == o + 8 * t + sub, 1.0, 0.0) for t in range(groups)]
    left = jnp.concatenate([rows[t] - eye[t] for t in range(groups)], 0)
    right = jnp.concatenate([jnp.where(inside, eye[t] - work[t], work[t]) for t in range(groups)], 0)
    m_ref[...] = m_ref[...] - outer(left, right)
    for t in range(groups):
        s = slice(o + 8 * t, o + 8 * t + 8)
        m_ref[s, :] = jnp.where(inside, -work[t], work[t])
        ft_ref[s, :] = jnp.where(lane >= o + 8 * t + sub, factor[t], 0.0)


def gather_kernel(
    mat_ref, panel, v_ref, ft, pc, pt, a00, s1, s2, sd, sp, sa, sb, rh, ro, ra, rp, lsem
):
    row = lax.axis_index("row")
    col = lax.axis_index("col")
    core = col % 2
    z = (col // 2) % NZ
    y = (col // 16) % NY
    x = col // 64
    mine = col // 2

    def block(bx, by, bz):
        return (bx * NY + by) * NZ + bz

    def device(r, bx, by, bz, k):
        return {"row": r, "col": block(bx, by, bz) * 2 + k}

    def shifted(q):
        return (x + q // NY) % NX, (y + q) % NY

    def push(src, dst, send, recv, to):
        return pltpu.make_async_remote_copy(
            src_ref=src, dst_ref=dst, send_sem=send, recv_sem=recv,
            device_id=to, device_id_type=pl.DeviceIdType.MESH,
        )

    own_half = pl.ds(core * HALF, HALF)
    h0, h1 = pl.ds(0, HALF), pl.ds(HALF, HALF)

    load = pltpu.make_async_copy(mat_ref.at[pl.ds(0, NB)], pc, lsem)

    @pl.when(row == 0)
    def _():
        load.start()

    barrier = pltpu.get_barrier_semaphore()

    def greet(to):
        pl.semaphore_signal(barrier, inc=1, device_id=to, device_id_type=pl.DeviceIdType.MESH)

    for d in range(1, NZ):
        greet(device(row, x, y, (z + d) % NZ, core))
    for q in range(NXY):
        qx, qy = shifted(q)
        if q:
            greet(device(row, qx, qy, z, core))
        greet(device(row, qx, qy, z, 1 - core))
        greet(device(1 - row, qx, qy, z, 1))
        greet(device(1 - row, qx, qy, z, 0))
    for d in range(1, NZ):
        greet(device(1 - row, x, y, (z + d) % NZ, 0))
        greet(device(1 - row, x, y, (z + d) % NZ, 1))
    expected = (NZ - 1) + (NXY - 1) + NXY + 2 * NXY + 2 * (NZ - 1)

    @pl.when(row == 0)
    def _():
        load.wait()
        pt[...] = pc[...].T

        @pl.when(core == 0)
        def _():
            panel[pl.ds(mine, 1), 0:HALF, :] = pt[0:HALF, :][None]

        @pl.when(col == 0)
        def _():
            a00[...] = pc[...]

    pl.semaphore_wait(barrier, expected)

    root = (row == 0) & (col == 0)

    def a00_h0(r, d):
        return push(a00.at[h0], a00.at[h0], sa.at[r * NZ + d], ra.at[0], device(r, 0, 0, d, 0))

    def a00_h1(r, q):
        return push(a00.at[h1], a00.at[h1], sa.at[16 + r * NXY + q], ra.at[1], device(r, q // NY, q % NY, 0, 1))

    def root_sends(act):
        for r in range(2):
            for d in range(NZ):
                if r or d:
                    act(a00_h0(r, d))
            for q in range(NXY):
                act(a00_h1(r, q))

    @pl.when(root)
    def _():
        root_sends(lambda c: c.start())

    def first_h0(d):
        return push(
            pt.at[h0], panel.at[mine, h0], s1.at[d], rh.at[mine], device(core, x, y, (z + d) % NZ, 0)
        )

    def first_h1(q):
        qx, qy = shifted(q)
        return push(pt.at[h1], panel.at[mine, h1], s1.at[NZ + q], rh.at[mine], device(core, qx, qy, z, 1))

    def pivot_rows():
        return push(pc, pc, sp.at[0], rp.at[0], device(1, x, y, z, core))

    def first_sends(act):
        for d in range(NZ):
            if d:
                act(first_h0(d))
            else:

                @pl.when(core == 1)
                def _():
                    act(first_h0(0))

            act(first_h1(d))
        act(pivot_rows())

    @pl.when(row == 0)
    def _():
        first_sends(lambda c: c.start())

    def across(i, half):
        return push(panel.at[i, half], panel.at[i, half], sd.at[i], ro.at[i], device(row, x, y, z, 1 - core))

    def arrived(i, half):
        push(panel.at[i, half], panel.at[i, half], sd.at[i], rh.at[i], device(row, x, y, z, 1 - core)).wait_recv()

    def step(t):
        return jnp.where(t % 2 == 1, (t + 1) // 2, NZ - t // 2)

    def a00_on0(q):
        qx, qy = q // NY, q % NY
        return push(a00.at[h0], a00.at[h0], sb.at[q], ra.at[0], device(row, qx, qy, z, 0))

    def a00_on1(d):
        return push(a00.at[h1], a00.at[h1], sb.at[d], ra.at[1], device(row, x, y, d, 1))

    def a00_across(half, k):
        return push(a00.at[half], a00.at[half], sb.at[8], ra.at[k], device(row, x, y, z, 1 - core))

    def second0(i, t, q):
        qx, qy = shifted(q)
        return push(panel.at[i, h0], panel.at[i, h0], s2.at[t * NXY + q], rh.at[i], device(row, qx, qy, z, 0))

    @pl.when(core == 0)
    def _():
        @pl.when(jnp.logical_not(root))
        def _():
            push(a00.at[h0], a00.at[h0], sb.at[8], ra.at[0], device(row, x, y, z, 1)).wait_recv()

        @pl.when((x == 0) & (y == 0))
        def _():
            for q in range(1, NXY):
                a00_on0(q).start()

        a00_across(h0, 0).start()

        @pl.loop(0, NZ)
        def _(t):
            i = block(x, y, (z + step(t)) % NZ)

            @pl.when((row == 1) | (t > 0))
            def _():
                arrived(i, h0)

            for q in range(1, NXY):
                second0(i, t, q).start()
            across(i, h0).start()

        @pl.loop(0, NZ)
        def _(t):
            for q in range(1, NXY):
                qx, qy = shifted(q)
                i = block(qx, qy, (z + step(t)) % NZ)
                arrived(i, h0)
                across(i, h0).start()

    def second1(i, s, q, way):
        to = device(row, x, y, (z + (1 if way == 0 else NZ - 1)) % NZ, 1)
        return push(panel.at[i, h1], panel.at[i, h1], s2.at[(s * 2 + way) * NXY + q], rh.at[i], to)

    @pl.when(core == 1)
    def _():
        @pl.loop(0, NXY)
        def _(q):
            qx, qy = shifted(q)
            i = block(qx, qy, z)
            arrived(i, h1)
            for way in range(2):
                second1(i, 0, q, way).start()
            across(i, h1).start()

        push(a00.at[h1], a00.at[h1], sb.at[8], ra.at[1], device(row, x, y, z, 0)).wait_recv()

        @pl.when(z == 0)
        def _():
            for d in range(1, NZ):
                a00_on1(d).start()

        @pl.when((row == 1) | (col != 1))
        def _():
            a00_across(h1, 1).start()

        for s in range(1, 4):

            @pl.loop(0, NXY)
            def _(q):
                qx, qy = shifted(q)
                for way in range(2):
                    i = block(qx, qy, (z + (NZ - s if way == 0 else s)) % NZ)
                    arrived(i, h1)
                    if s < 3:
                        second1(i, s, q, way).start()
                    else:

                        @pl.when((qx + qy) % 2 == way)
                        def _():
                            second1(i, s, q, way).start()

                    across(i, h1).start()

        @pl.loop(0, NXY)
        def _(q):
            qx, qy = shifted(q)
            i = block(qx, qy, (z + 4) % NZ)
            arrived(i, h1)
            across(i, h1).start()

    @pl.when((core == 0) & jnp.logical_not(root))
    def _():
        push(a00.at[h1], a00.at[h1], sb.at[8], ra.at[1], device(row, x, y, z, 1)).wait_recv()

    @pl.when(core == 1)
    def _():
        push(a00.at[h0], a00.at[h0], sb.at[8], ra.at[0], device(row, x, y, z, 0)).wait_recv()

    @pl.when(row == 1)
    def _():
        push(pc, pc, sp.at[0], rp.at[0], device(0, x, y, z, core)).wait_recv()

    v_ref[...] = a00[...]
    for k in range(NB // PIVOTS):
        sweep_block(v_ref, ft, k)
    minus_inverse = v_ref[...]
    first = jnp.broadcast_to(col, (NB, NB)) == 0
    rhs = jnp.where(first, -ft[...].T, pc[...])
    v_ref[...] = jnp.dot(minus_inverse, rhs, precision=lax.Precision.HIGHEST, preferred_element_type=F32)

    @pl.loop(0, BLOCKS)
    def _(i):
        other = pl.ds((1 - core) * HALF, HALF)
        push(panel.at[i, other], panel.at[i, other], sd.at[i], ro.at[i], device(row, x, y, z, 1 - core)).wait_recv()

    @pl.loop(0, BLOCKS)
    def _(i):
        across(i, own_half).wait_send()

    @pl.when(root)
    def _():
        root_sends(lambda c: c.wait_send())

    @pl.when(row == 0)
    def _():
        first_sends(lambda c: c.wait_send())

    @pl.when(core == 0)
    def _():
        @pl.when((x == 0) & (y == 0))
        def _():
            for q in range(1, NXY):
                a00_on0(q).wait_send()

        a00_across(h0, 0).wait_send()

        @pl.loop(0, NZ)
        def _(t):
            i = block(x, y, (z + step(t)) % NZ)
            for q in range(1, NXY):
                second0(i, t, q).wait_send()

    @pl.when(core == 1)
    def _():
        @pl.when(z == 0)
        def _():
            for d in range(1, NZ):
                a00_on1(d).wait_send()

        @pl.when((row == 1) | (col != 1))
        def _():
            a00_across(h1, 1).wait_send()

        for s in range(4):

            @pl.loop(0, NXY)
            def _(q):
                qx, qy = shifted(q)
                for way in range(2):
                    i = block(qx, qy, (z + (NZ - s if way == 0 else s)) % NZ)
                    if s < 3:
                        second1(i, s, q, way).wait_send()
                    else:

                        @pl.when((qx + qy) % 2 == way)
                        def _():
                            second1(i, s, q, way).wait_send()


def update_kernel(chunk, panel_ref, mat_ref, v_ref, ft_ref, out_ref):
    first = lax.axis_index("col") == 0
    keep = jnp.where(first, 0.0, 1.0)
    rows = panel_ref[...].reshape(chunk * NB, NB)
    moved = jnp.dot(rows, v_ref[...], precision=lax.Precision.HIGHEST, preferred_element_type=F32)
    out_ref[...] = mat_ref[...] * keep + moved

    @pl.when((pl.program_id(0) == 0) & (lax.axis_index("row") == 0))
    def _():
        out_ref[0:NB, :] = jnp.where(jnp.broadcast_to(lax.axis_index("col"), (NB, NB)) == 0, ft_ref[...].T, mat_ref[0:NB, :])


def on_device(matrix):
    shape = matrix.shape
    local = matrix.reshape(BLOCKS * NB, NB)
    whole = pl.BlockSpec(memory_space=pltpu.VMEM)
    dma = pltpu.SemaphoreType.DMA
    panel, v, ft = pl.pallas_call(
        gather_kernel,
        out_shape=[
            jax.ShapeDtypeStruct((BLOCKS, NB, NB), F32),
            jax.ShapeDtypeStruct((NB, NB), F32),
            jax.ShapeDtypeStruct((NB, NB), F32),
        ],
        in_specs=[pl.BlockSpec(memory_space=pltpu.HBM)],
        out_specs=[whole, whole, whole],
        scratch_shapes=[pltpu.VMEM((NB, NB), F32)] * 3
        + [dma((16,)), dma((64,)), dma((64,)), dma((1,)), dma((32,)), dma((9,))]
        + [dma((64,)), dma((64,)), dma((2,)), dma((1,)), dma],
        compiler_params=pltpu.CompilerParams(
            collective_id=0, has_side_effects=True, vmem_limit_bytes=24 << 20
        ),
        name="gather",
    )(local)
    chunk = 4
    out = pl.pallas_call(
        functools.partial(update_kernel, chunk),
        grid=(BLOCKS // chunk,),
        out_shape=jax.ShapeDtypeStruct((BLOCKS * NB, NB), F32),
        in_specs=[
            pl.BlockSpec((chunk, NB, NB), lambda i: (i, 0, 0)),
            pl.BlockSpec((chunk * NB, NB), lambda i: (i, 0)),
            pl.BlockSpec((NB, NB), lambda i: (0, 0)),
            pl.BlockSpec((NB, NB), lambda i: (0, 0)),
        ],
        out_specs=pl.BlockSpec((chunk * NB, NB), lambda i: (i, 0)),
        name="update",
    )(panel, local, v, ft)
    return out.reshape(shape)


def solution(mesh):
    spec = P(None, "row", None, None, "col", None)
    return jax.shard_map(on_device, mesh=mesh, in_specs=(spec,), out_specs=spec, check_vma=False)
```

```python
import functools

import jax
import jax.numpy as jnp
from jax import lax
from jax.experimental import pallas as pl
from jax.experimental.pallas import tpu as pltpu
from jax.sharding import PartitionSpec as P

F32 = jnp.float32
BF16 = jnp.bfloat16
NB = 128
HALF = NB // 2
BLOCKS = 64
NX, NY, NZ = 2, 4, 8
NXY = NX * NY
PIVOTS = 16
VMEM_LIMIT = 56 << 20


def split3(x):
    first = x.astype(BF16)
    rest = x - first.astype(F32)
    second = rest.astype(BF16)
    return first, second, (rest - second.astype(F32)).astype(BF16)


def outer(u, t):
    u1, u2, u3 = split3(u)
    t1, t2, t3 = split3(t)
    left = jnp.concatenate([u1, u1, u2, u2, u1, u3], 0)
    right = jnp.concatenate([t1, t2, t1, t2, t3, t1], 0)
    return lax.dot_general(left, right, (((0,), (0,)), ((), ())), preferred_element_type=F32)


def sweep_block(m_ref, ft_ref, block):
    b = PIVOTS
    groups = b // 8
    o = block * b
    sub = lax.broadcasted_iota(jnp.int32, (8, NB), 0)
    lane = lax.broadcasted_iota(jnp.int32, (8, NB), 1)
    rows = [m_ref[o + 8 * t : o + 8 * t + 8, :] for t in range(groups)]
    work = list(rows)
    cols = [[jnp.broadcast_to(rows[t][:, o + j : o + j + 1], (8, NB)) for t in range(groups)] for j in range(b)]
    factor = [None] * groups
    for j in range(b):
        tj, sj = divmod(j, 8)
        pivot = cols[j][tj][sj : sj + 1, :]
        inverse = 1.0 / pivot
        line = work[tj][sj : sj + 1, :] * lax.rsqrt(pivot)
        factor[tj] = jnp.broadcast_to(line, (8, NB)) if sj == 0 else jnp.where(sub == sj, line, factor[tj])
        work = [
            jnp.where(lane == o + j, jnp.where(sub == sj, 1.0, 0.0) if t == tj else 0.0, work[t])
            for t in range(groups)
        ]
        by = list(cols[j])
        by[tj] = jnp.where(sub == sj, cols[j][tj] - 1.0, cols[j][tj])
        scaled = work[tj][sj : sj + 1, :] * inverse
        work = [work[t] - by[t] * scaled for t in range(groups)]
        for m in range(j + 1, b):
            one = cols[m][tj][sj : sj + 1, :] * inverse
            cols[m] = [cols[m][t] - by[t] * one for t in range(groups)]
    inside = (lane >= o) & (lane < o + b)
    eye = [jnp.where(lane == o + 8 * t + sub, 1.0, 0.0) for t in range(groups)]
    left = jnp.concatenate([rows[t] - eye[t] for t in range(groups)], 0)
    right = jnp.concatenate([jnp.where(inside, eye[t] - work[t], work[t]) for t in range(groups)], 0)
    m_ref[...] = m_ref[...] - outer(left, right)
    for t in range(groups):
        s = slice(o + 8 * t, o + 8 * t + 8)
        m_ref[s, :] = jnp.where(inside, -work[t], work[t])
        ft_ref[s, :] = jnp.where(lane >= o + 8 * t + sub, factor[t], 0.0)


def step_kernel(
    mat_ref, out_ref, panel, mine_ref, v_ref, ft, pc, pt, a00, nv, weights,
    s1, sz, s2, sd, sa, sp, r1, r2, ro, ra, rp, lsem
):
    row = lax.axis_index("row")
    col = lax.axis_index("col")
    core = lax.rem(col, 2)
    z = lax.rem(lax.div(col, 2), NZ)
    y = lax.rem(lax.div(col, 2 * NZ), NY)
    x = lax.div(col, 2 * NZ * NY)

    def wrap(v, n):
        return jnp.where(v >= n, v - n, v)

    xs = [x, 1 - x]
    ys = [wrap(y + d, NY) for d in range(NY)]
    zs = [wrap(z + d, NZ) for d in range(NZ)]
    offsets = [(1, 2), (1, 1), (1, 3), (0, 2), (1, 0), (0, 1), (0, 3)]
    line = [0, 1, 7, 2, 6, 3, 5, 4]

    def device(r, bx, by, bz, k):
        return {"row": r, "col": bx * (2 * NZ * NY) + by * (2 * NZ) + bz * 2 + k}

    def at(qx, qy):
        return xs[qx % NX] * NY + ys[qy % NY]

    here = at(0, 0)

    def push(src, dst, send, recv, to):
        return pltpu.make_async_remote_copy(
            src_ref=src, dst_ref=dst, send_sem=send, recv_sem=recv,
            device_id=to, device_id_type=pl.DeviceIdType.MESH,
        )

    sibling = device(row, x, y, z, 1 - core)

    def wait_bytes(ref, sem):
        push(ref, ref, sem, sem, sibling).wait_recv()

    def wait_sent(ref, sem):
        push(ref, ref, sem, sem, sibling).wait_send()

    h0, h1 = pl.ds(0, HALF), pl.ds(HALF, HALF)
    root = (row == 0) & (col == 0)

    load = pltpu.make_async_copy(mat_ref.at[0, 0], pc, lsem.at[0])
    load_all = pltpu.make_async_copy(mat_ref, mine_ref, lsem.at[1])

    @pl.when(row == 0)
    def _():
        load.start()

    load_all.start()

    barrier = pltpu.get_barrier_semaphore()

    def greet(to):
        pl.semaphore_signal(barrier, inc=1, device_id=to, device_id_type=pl.DeviceIdType.MESH)

    greet(sibling)
    greet(device(1 - row, x, y, z, core))
    for d in (1, NZ - 1):
        greet(device(row, x, y, zs[d], core))

    @pl.when(core == 0)
    def _():
        for d in range(2, NZ - 1):
            greet(device(row, x, y, zs[d], 0))
        for qx, qy in offsets:
            greet(device(row, xs[qx], ys[qy], z, 0))

    @pl.when(core == 1)
    def _():
        for qx, qy in offsets:
            greet(device(1 - row, xs[qx], ys[qy], z, 1))

    @pl.when(row == 0)
    def _():
        for qx, qy in offsets:
            greet(device(0, xs[qx], ys[qy], z, 1 - core))

    @pl.when(row != core)
    def _():
        for qx in range(NX):
            greet(device(1 - row, xs[qx], y, z, 1 - core))

    @pl.when(root)
    def _():
        for q in range(1, NXY):
            greet(device(1, q // NY, q % NY, 0, 0))

    @pl.when((row == 1) & (core == 0) & (z == 0) & (here > 0))
    def _():
        greet(device(0, 0, 0, 0, 0))

    heard = 4 + (NZ - 3 + NXY - 1) * (1 - core) + (NXY - 1) * core + (NXY - 1) * (1 - row)
    heard += jnp.where(row != core, NX, 0) + jnp.where(root, NXY - 1, 0)
    heard += jnp.where((row == 1) & (core == 0) & (z == 0) & (here > 0), 1, 0)

    @pl.when(row == 0)
    def _():
        load.wait()
        pt[...] = pc[...].T

        @pl.when(core == 0)
        def _():
            panel[pl.ds(here, 1), pl.ds(z, 1), 0:HALF, :] = pt[0:HALF, :][None, None]

        @pl.when(col == 0)
        def _():
            a00[...] = pc[...]

    pl.semaphore_wait(barrier, heard)

    def a00_push(i, to):
        return push(a00, a00, sa.at[i], ra.at[0], to)

    def root_sends(act):
        for n, d in enumerate([4, 3, 5, 2, 6, 1, 7]):
            act(a00_push(n, device(0, 0, 0, d, 0)))
        for n, q in enumerate([6, 5, 7, 2, 4, 1, 3, 0]):
            act(a00_push(7 + n, device(1, q // NY, q % NY, 0, 0)))

    def second_sends(act):
        @pl.when((row == 0) & (here == 0))
        def _():
            for n, (qx, qy) in enumerate(offsets):
                act(a00_push(15 + n, device(0, qx, qy, z, 0)))

        @pl.when((row == 1) & (z == 0))
        def _():
            for n, d in enumerate([4, 3, 5, 2, 6, 1, 7]):
                act(a00_push(15 + n, device(1, x, y, d, 0)))

    def a00_wait():
        @pl.when(jnp.logical_not(root))
        def _():
            wait_bytes(a00, ra.at[0])

    @pl.when(root)
    def _():
        root_sends(lambda c: c.start())
        second_sends(lambda c: c.start())

    def cross(d, half):
        group = panel.at[:, zs[d], half]
        push(group, group, sd.at[0], ro.at[d], sibling).start()

    def set_weights(rhs, minus_inverse):
        v = jnp.dot(minus_inverse[...], rhs, precision=lax.Precision.HIGHEST, preferred_element_type=F32)
        high = v.astype(BF16)
        low = (v - high.astype(F32)).astype(BF16)
        both = jnp.concatenate([high, low], 1)
        weights[...] = jnp.concatenate([both, both], 0)

    keep = jnp.where(col == 0, 0.0, 1.0)

    def update(d, half):
        there = (slice(None), pl.ds(zs[d], 1), slice(half * HALF, (half + 1) * HALF), slice(None))
        rows = panel[there].reshape(NXY * HALF, NB)
        high = rows.astype(BF16)
        low = (rows - high.astype(F32)).astype(BF16)
        parts = jnp.dot(jnp.concatenate([high, low], 1), weights[...], preferred_element_type=F32)
        moved = (parts[:, :NB] + parts[:, NB:]).reshape(NXY, 1, HALF, NB)
        out_ref[there] = mine_ref[there] * keep + moved

    def along_z(src, q, d):
        return push(src, panel.at[at(q, 0), z, h0], sz.at[0], r1.at[q * NZ + d], device(row, x, y, zs[-d % NZ], 0))

    def first_x(q):
        return push(pt.at[h0], panel.at[here, z, h0], s1.at[0], r1.at[q * NZ], device(core, xs[q], y, z, 0))

    def first_h1(n, qx, qy):
        return push(pt.at[h1], panel.at[here, z, h1], s1.at[0], r1.at[n], device(core, xs[qx], ys[qy], z, 1))

    def pivot_rows():
        return push(pc, pc, sp.at[0], rp.at[0], device(1, x, y, z, core))

    @pl.when(row == 0)
    def _():
        first_x(1).start()

        @pl.when(core == 1)
        def _():
            first_x(0).start()

        first_h1(7, 0, 0).start()
        for n in range(NXY - 1):
            first_h1(n, *offsets[n]).start()

            @pl.when(core == 0)
            def _():
                along_z(pt.at[h0], 0, line[n + 1]).start()

        pivot_rows().start()

    @pl.when(core == 0)
    def _():
        def along_y(q, d):
            piece = panel.at[at(q, 0), zs[d], h0]
            for qy in (2, 1, 3):
                push(piece, piece, s2.at[0], r2.at[d], device(row, x, ys[qy], z, 0)).start()

        def wait_line(q, d):
            wait_bytes(pt.at[h0], r1.at[q * NZ + d])

        def spread(q):
            for d in line[1:]:
                along_z(panel.at[at(q, 0), z, h0], q, d).start()

        @pl.when(row == 1)
        def _():
            wait_line(0, 0)
            spread(0)

        along_y(0, 0)
        wait_line(1, 0)
        spread(1)
        along_y(1, 0)

        def a00_on():
            @pl.when(((row == 0) & (here == 0) & (col > 0)) | ((row == 1) & (z == 0)))
            def _():
                wait_bytes(a00, ra.at[0])
                second_sends(lambda c: c.start())

        for n, d in enumerate(line[1:]):
            wait_line(0, d)
            along_y(0, d)
            if n == 1:
                a00_on()
        for d in line[1:]:
            wait_line(1, d)
            along_y(1, d)
        @pl.when(jnp.logical_not(((row == 0) & (here == 0)) | ((row == 1) & (z == 0))))
        def _():
            wait_bytes(a00, ra.at[0])
        @pl.when(row == 1)
        def _():
            wait_bytes(pc, rp.at[0])

        load_all.wait()
        v_ref[...] = a00[...]
        for n in range(NB // PIVOTS):
            sweep_block(v_ref, ft, n)
        push(v_ref, nv, sp.at[1], rp.at[1], sibling).start()
        first = jnp.broadcast_to(col, (NB, NB)) == 0
        set_weights(jnp.where(first, -ft[...].T, pc[...]), v_ref)

        for n, d in enumerate(line):
            wait_bytes(panel.at[pl.ds(0, NXY - 2), 0, h0], r2.at[d])
            cross(d, h0)
            update(d, 0)

    @pl.when(core == 1)
    def _():
        sources = [(0, 0)] + [(-qx, -qy) for qx, qy in offsets]
        sems = [7, 0, 1, 2, 3, 4, 5, 6]

        def ring(i, s, n, way):
            piece = panel.at[i, zs[-s % NZ] if way == 0 else zs[s], h1]
            to = device(row, x, y, zs[1] if way == 0 else zs[7], 1)
            return push(piece, piece, s2.at[0], r2.at[(s * 2 + way) * NXY + n], to)

        for n, (qx, qy) in enumerate(sources):
            i = at(qx, qy)
            wait_bytes(panel.at[i, z, h1], r1.at[sems[n]])
            for way in range(2):
                ring(i, 0, n, way).start()
        cross(0, h1)
        for s in range(1, 4):
            for n, (qx, qy) in enumerate(sources):
                i = at(qx, qy)
                for way in range(2):
                    wait_bytes(panel.at[i, z, h1], r2.at[((s - 1) * 2 + way) * NXY + n])
                    if s < 3:
                        ring(i, s, n, way).start()
                    elif n % 2 == way:
                        ring(i, s, n, way).start()
            cross(-s % NZ, h1)
            cross(s, h1)
        for n, (qx, qy) in enumerate(sources):
            i = at(qx, qy)
            wait_bytes(panel.at[i, z, h1], r2.at[(3 * 2 + n % 2) * NXY + n])
        cross(4, h1)

        @pl.when(row == 1)
        def _():
            wait_bytes(pc, rp.at[0])
        load_all.wait()
        wait_bytes(nv, rp.at[1])
        set_weights(pc[...], nv)
        for d in line:
            update(d, 1)

    @pl.when(core == 0)
    def _():
        for d in line:
            wait_bytes(panel.at[:, 0, h0], ro.at[d])
            update(d, 1)

    @pl.when(core == 1)
    def _():
        for d in line:
            wait_bytes(panel.at[:, 0, h0], ro.at[d])
            update(d, 0)

    @pl.when(row == 0)
    def _():
        head = mine_ref[0, 0]
        out_ref[0, 0] = jnp.where(jnp.broadcast_to(col, (NB, NB)) == 0, ft[...].T, head)

    wait_sent(panel.at[:, :, h0], sd.at[0])

    @pl.when(core == 0)
    def _():
        wait_sent(v_ref, sp.at[1])

    @pl.when(root)
    def _():
        root_sends(lambda c: c.wait_send())

    @pl.when(core == 0)
    def _():
        second_sends(lambda c: c.wait_send())
    @pl.when(row == 0)
    def _():
        wait_sent(panel.at[0, :, h0], s1.at[0])
        wait_sent(pt.at[h0], s1.at[0])

        @pl.when(core == 1)
        def _():
            wait_sent(pt.at[h0], s1.at[0])

        wait_sent(pc, sp.at[0])

    @pl.when(core == 0)
    def _():
        wait_sent(panel.at[pl.ds(0, 2), pl.ds(0, NZ - 1), h0], sz.at[0])
        wait_sent(panel.at[pl.ds(0, 6), :, h0], s2.at[0])
    @pl.when(core == 1)
    def _():
        wait_sent(panel.at[pl.ds(0, NXY - 1), :, h0], s2.at[0])


def on_device_gather(matrix):
    shape = (NXY, NZ, NB, NB)
    dma = pltpu.SemaphoreType.DMA
    block = pltpu.VMEM((NB, NB), F32)
    return pl.pallas_call(
        step_kernel,
        out_shape=pltpu.VMEM(shape, F32),
        in_specs=[pl.BlockSpec(memory_space=pltpu.HBM)],
        out_specs=pl.BlockSpec(memory_space=pltpu.VMEM),
        scratch_shapes=[pltpu.VMEM(shape, F32)] * 2
        + [block] * 6
        + [pltpu.VMEM((2 * NB, 2 * NB), BF16)]
        + [dma((1,)), dma((1,)), dma((1,)), dma((1,)), dma((22,)), dma((2,))]
        + [dma((16,)), dma((64,)), dma((8,)), dma((1,)), dma((2,)), dma((2,))],
        compiler_params=pltpu.CompilerParams(
            collective_id=0, has_side_effects=True, vmem_limit_bytes=VMEM_LIMIT
        ),
        name="step",
    )(matrix)


def on_device(matrix):
    local = matrix.reshape(NXY, NZ, NB, NB)
    return on_device_gather(local).reshape(matrix.shape)


def solution(mesh):
    spec = P(None, "row", None, None, "col", None)
    return jax.shard_map(on_device, mesh=mesh, in_specs=(spec,), out_specs=spec, check_vma=False)
```

```python
import functools

import jax
import jax.numpy as jnp
from jax import lax
from jax.experimental import pallas as pl
from jax.experimental.pallas import tpu as pltpu
from jax.sharding import PartitionSpec as P

F32 = jnp.float32
BF16 = jnp.bfloat16
NB = 128
HALF = NB // 2
HA = 56
BLOCKS = 64
NX, NY, NZ = 2, 4, 8
NXY = NX * NY
PIVOTS = 16
VMEM_LIMIT = 56 << 20


def split3(x):
    first = x.astype(BF16)
    rest = x - first.astype(F32)
    second = rest.astype(BF16)
    return first, second, (rest - second.astype(F32)).astype(BF16)


def outer(u, t):
    u1, u2, u3 = split3(u)
    t1, t2, t3 = split3(t)
    left = jnp.concatenate([u1, u1, u2, u2, u1, u3], 0)
    right = jnp.concatenate([t1, t2, t1, t2, t3, t1], 0)
    return lax.dot_general(left, right, (((0,), (0,)), ((), ())), preferred_element_type=F32)


def sweep_block(m_ref, ft_ref, block):
    b = PIVOTS
    groups = b // 8
    o = block * b
    sub = lax.broadcasted_iota(jnp.int32, (8, NB), 0)
    lane = lax.broadcasted_iota(jnp.int32, (8, NB), 1)
    rows = [m_ref[o + 8 * t : o + 8 * t + 8, :] for t in range(groups)]
    work = list(rows)
    cols = [[jnp.broadcast_to(rows[t][:, o + j : o + j + 1], (8, NB)) for t in range(groups)] for j in range(b)]
    factor = [None] * groups
    for j in range(b):
        tj, sj = divmod(j, 8)
        pivot = cols[j][tj][sj : sj + 1, :]
        inverse = 1.0 / pivot
        line = work[tj][sj : sj + 1, :] * lax.rsqrt(pivot)
        factor[tj] = jnp.broadcast_to(line, (8, NB)) if sj == 0 else jnp.where(sub == sj, line, factor[tj])
        work = [
            jnp.where(lane == o + j, jnp.where(sub == sj, 1.0, 0.0) if t == tj else 0.0, work[t])
            for t in range(groups)
        ]
        by = list(cols[j])
        by[tj] = jnp.where(sub == sj, cols[j][tj] - 1.0, cols[j][tj])
        scaled = work[tj][sj : sj + 1, :] * inverse
        work = [work[t] - by[t] * scaled for t in range(groups)]
        for m in range(j + 1, b):
            one = cols[m][tj][sj : sj + 1, :] * inverse
            cols[m] = [cols[m][t] - by[t] * one for t in range(groups)]
    inside = (lane >= o) & (lane < o + b)
    eye = [jnp.where(lane == o + 8 * t + sub, 1.0, 0.0) for t in range(groups)]
    left = jnp.concatenate([rows[t] - eye[t] for t in range(groups)], 0)
    right = jnp.concatenate([jnp.where(inside, eye[t] - work[t], work[t]) for t in range(groups)], 0)
    m_ref[...] = m_ref[...] - outer(left, right)
    for t in range(groups):
        s = slice(o + 8 * t, o + 8 * t + 8)
        m_ref[s, :] = jnp.where(inside, -work[t], work[t])
        ft_ref[s, :] = jnp.where(lane >= o + 8 * t + sub, factor[t], 0.0)


def pack(block):
    sub = lax.broadcasted_iota(jnp.int32, (HALF, NB), 0)
    lane = lax.broadcasted_iota(jnp.int32, (HALF, NB), 1)
    top, bottom = block[:HALF], block[HALF:]
    body = jnp.where(sub > lane, pltpu.roll(bottom, HALF, 1), top)
    diagonal = jnp.sum(jnp.where(lane == sub + HALF, bottom, 0.0), axis=0, keepdims=True)
    return jnp.concatenate([body, jnp.broadcast_to(diagonal, (8, NB))], 0)


def unpack(ref):
    sub = lax.broadcasted_iota(jnp.int32, (HALF, NB), 0)
    lane = lax.broadcasted_iota(jnp.int32, (HALF, NB), 1)
    body = ref[0:HALF, :]
    last = pltpu.roll(jnp.where(sub > lane, body, 0.0), HALF, 1)
    strict = jnp.concatenate([jnp.where(sub < lane, body, 0.0), last], 0)
    diagonal = jnp.broadcast_to(ref[HALF : HALF + 1, :], (HALF, NB))
    diagonal = jnp.concatenate(
        [jnp.where(sub == lane, body, 0.0), jnp.where(lane == sub + HALF, diagonal, 0.0)], 0
    )
    return strict + strict.T + diagonal


def step_kernel(
    mat_ref, out_ref, panel, mine_ref, v_ref, ft, pc, pt, packed, nv, weights,
    s1, sz, s2, sd, sa, sp, r1, r2, ro, ra, rp, lsem
):
    row = lax.axis_index("row")
    col = lax.axis_index("col")
    core = lax.rem(col, 2)
    z = lax.rem(lax.div(col, 2), NZ)
    y = lax.rem(lax.div(col, 2 * NZ), NY)
    x = lax.div(col, 2 * NZ * NY)

    def wrap(v, n):
        return jnp.where(v >= n, v - n, v)

    xs = [x, 1 - x]
    ys = [wrap(y + d, NY) for d in range(NY)]
    zs = [wrap(z + d, NZ) for d in range(NZ)]
    offsets = [(1, 2), (1, 1), (1, 3), (0, 2), (1, 0), (0, 1), (0, 3)]
    line = [0, 1, 7, 2, 6, 3, 5, 4]

    def device(r, bx, by, bz, k):
        return {"row": r, "col": bx * (2 * NZ * NY) + by * (2 * NZ) + bz * 2 + k}

    def at(qx, qy):
        return xs[qx % NX] * NY + ys[qy % NY]

    here = at(0, 0)

    def push(src, dst, send, recv, to):
        return pltpu.make_async_remote_copy(
            src_ref=src, dst_ref=dst, send_sem=send, recv_sem=recv,
            device_id=to, device_id_type=pl.DeviceIdType.MESH,
        )

    sibling = device(row, x, y, z, 1 - core)

    def wait_bytes(ref, sem):
        push(ref, ref, sem, sem, sibling).wait_recv()

    def wait_sent(ref, sem):
        push(ref, ref, sem, sem, sibling).wait_send()

    h0, h1 = pl.ds(0, HA), pl.ds(HA, NB - HA)
    root = (row == 0) & (col == 0)

    load = pltpu.make_async_copy(mat_ref.at[0, 0], pc, lsem.at[0])
    load_all = pltpu.make_async_copy(mat_ref, mine_ref, lsem.at[1])

    @pl.when(row == 0)
    def _():
        load.start()

    load_all.start()

    barrier = pltpu.get_barrier_semaphore()

    def greet(to):
        pl.semaphore_signal(barrier, inc=1, device_id=to, device_id_type=pl.DeviceIdType.MESH)

    greet(sibling)
    greet(device(1 - row, x, y, z, core))
    for d in (1, NZ - 1):
        greet(device(row, x, y, zs[d], core))

    @pl.when(core == 0)
    def _():
        for d in range(2, NZ - 1):
            greet(device(row, x, y, zs[d], 0))
        for qx, qy in offsets:
            greet(device(row, xs[qx], ys[qy], z, 0))

    @pl.when(core == 1)
    def _():
        for qx, qy in offsets:
            greet(device(1 - row, xs[qx], ys[qy], z, 1))

    @pl.when(row == 0)
    def _():
        for qx, qy in offsets:
            greet(device(0, xs[qx], ys[qy], z, 1 - core))

    @pl.when(row != core)
    def _():
        for qx in range(NX):
            greet(device(1 - row, xs[qx], y, z, 1 - core))

    @pl.when(root)
    def _():
        for q in range(1, NXY):
            greet(device(1, q // NY, q % NY, 0, 0))

    @pl.when((row == 1) & (core == 0) & (z == 0) & (here > 0))
    def _():
        greet(device(0, 0, 0, 0, 0))

    heard = 4 + (NZ - 3 + NXY - 1) * (1 - core) + (NXY - 1) * core + (NXY - 1) * (1 - row)
    heard += jnp.where(row != core, NX, 0) + jnp.where(root, NXY - 1, 0)
    heard += jnp.where((row == 1) & (core == 0) & (z == 0) & (here > 0), 1, 0)

    @pl.when(row == 0)
    def _():
        load.wait()
        pt[...] = pc[...].T

        @pl.when(core == 0)
        def _():
            panel[pl.ds(here, 1), pl.ds(z, 1), 0:HA, :] = pt[0:HA, :][None, None]

        @pl.when(col == 0)
        def _():
            packed[...] = pack(pc[...])

    pl.semaphore_wait(barrier, heard)

    def a00_push(i, to):
        return push(packed, packed, sa.at[i], ra.at[0], to)

    def root_sends(act):
        for n, d in enumerate([4, 3, 5, 2, 6, 1, 7]):
            act(a00_push(n, device(0, 0, 0, d, 0)))
        for n, q in enumerate([6, 5, 7, 2, 4, 1, 3, 0]):
            act(a00_push(7 + n, device(1, q // NY, q % NY, 0, 0)))

    def second_sends(act):
        @pl.when((row == 0) & (here == 0))
        def _():
            for n, (qx, qy) in enumerate(offsets):
                act(a00_push(15 + n, device(0, qx, qy, z, 0)))

        @pl.when((row == 1) & (z == 0))
        def _():
            for n, d in enumerate([4, 3, 5, 2, 6, 1, 7]):
                act(a00_push(15 + n, device(1, x, y, d, 0)))

    @pl.when(root)
    def _():
        root_sends(lambda c: c.start())
        second_sends(lambda c: c.start())

    def cross(d, half):
        group = panel.at[:, zs[d], half]
        push(group, group, sd.at[0], ro.at[d], sibling).start()

    def set_weights(rhs, minus_inverse):
        v = jnp.dot(minus_inverse[...], rhs, precision=lax.Precision.HIGHEST, preferred_element_type=F32)
        high = v.astype(BF16)
        low = (v - high.astype(F32)).astype(BF16)
        both = jnp.concatenate([high, low], 1)
        weights[...] = jnp.concatenate([both, both], 0)

    keep = jnp.where(col == 0, 0.0, 1.0)

    def update(d, start, size):
        there = (slice(None), pl.ds(zs[d], 1), slice(start, start + size), slice(None))
        rows = panel[there].reshape(NXY * size, NB)
        high = rows.astype(BF16)
        low = (rows - high.astype(F32)).astype(BF16)
        parts = jnp.dot(jnp.concatenate([high, low], 1), weights[...], preferred_element_type=F32)
        moved = (parts[:, :NB] + parts[:, NB:]).reshape(NXY, 1, size, NB)
        out_ref[there] = mine_ref[there] * keep + moved

    def update0(d):
        update(d, 0, HA)

    def update1(d):
        update(d, HA, NB - HA)

    def along_z(src, q, d):
        return push(src, panel.at[at(q, 0), z, h0], sz.at[0], r1.at[q * NZ + d], device(row, x, y, zs[-d % NZ], 0))

    def first_x(q):
        return push(pt.at[h0], panel.at[here, z, h0], s1.at[0], r1.at[q * NZ], device(core, xs[q], y, z, 0))

    def first_h1(n, qx, qy):
        return push(pt.at[h1], panel.at[here, z, h1], s1.at[1], r1.at[n], device(core, xs[qx], ys[qy], z, 1))

    def pivot_rows():
        return push(pc, pc, sp.at[0], rp.at[0], device(1, x, y, z, core))

    @pl.when(row == 0)
    def _():
        @pl.when(core == 1)
        def _():
            first_x(0).start()

        first_x(1).start()
        first_h1(7, 0, 0).start()
        for n in range(NXY - 1):
            first_h1(n, *offsets[n]).start()

            @pl.when(core == 0)
            def _():
                along_z(pt.at[h0], 0, line[n + 1]).start()

    @pl.when(core == 0)
    def _():
        def along_y(q, d):
            piece = panel.at[at(q, 0), zs[d], h0]
            for qy in (2, 1, 3):
                push(piece, piece, s2.at[0], r2.at[d], device(row, x, ys[qy], z, 0)).start()

        def wait_line(q, d):
            wait_bytes(pt.at[h0], r1.at[q * NZ + d])

        def spread(q):
            for d in line[1:]:
                along_z(panel.at[at(q, 0), z, h0], q, d).start()

        @pl.when(row == 1)
        def _():
            wait_line(0, 0)
            spread(0)

        along_y(0, 0)
        wait_line(1, 0)
        spread(1)
        along_y(1, 0)

        def a00_on():
            @pl.when(((row == 0) & (here == 0) & (col > 0)) | ((row == 1) & (z == 0)))
            def _():
                wait_bytes(packed, ra.at[0])
                second_sends(lambda c: c.start())

        for n, d in enumerate(line[1:]):
            wait_line(0, d)
            along_y(0, d)
            if n == 1:
                a00_on()

        @pl.when(row == 0)
        def _():
            pivot_rows().start()

        for d in line[1:]:
            wait_line(1, d)
            along_y(1, d)

        @pl.when(jnp.logical_not(((row == 0) & (here == 0)) | ((row == 1) & (z == 0))))
        def _():
            wait_bytes(packed, ra.at[0])
        def group(n):
            wait_bytes(panel.at[pl.ds(0, NXY - 2), 0, h0], r2.at[line[n]])
            cross(line[n], h0)

        def other(d):
            wait_bytes(panel.at[:, 0, h1], ro.at[d])
            update1(d)

        v_ref[...] = unpack(packed)
        done = 0
        for n in range(NB // PIVOTS):
            sweep_block(v_ref, ft, n)
            if n >= 3:
                group(done)
                done += 1
        push(v_ref, nv, sp.at[1], rp.at[1], sibling).start()

        @pl.when(row == 1)
        def _():
            wait_bytes(pc, rp.at[0])

        first = jnp.broadcast_to(col, (NB, NB)) == 0
        set_weights(jnp.where(first, -ft[...].T, pc[...]), v_ref)
        load_all.wait()
        for n in range(done):
            update0(line[n])
        for d in line[:3]:
            other(d)
        for n in range(done, NZ):
            group(n)
            update0(line[n])
        for d in line[3:]:
            other(d)

    @pl.when(core == 1)
    def _():
        sources = [(0, 0)] + [(-qx, -qy) for qx, qy in offsets]
        sems = [7, 0, 1, 2, 3, 4, 5, 6]

        def ring(i, s, n, way):
            piece = panel.at[i, zs[-s % NZ] if way == 0 else zs[s], h1]
            to = device(row, x, y, zs[1] if way == 0 else zs[7], 1)
            return push(piece, piece, s2.at[0], r2.at[(s * 2 + way) * NXY + n], to)

        for n, (qx, qy) in enumerate(sources):
            i = at(qx, qy)
            wait_bytes(panel.at[i, z, h1], r1.at[sems[n]])
            for way in range(2):
                ring(i, 0, n, way).start()
        cross(0, h1)

        @pl.when(row == 0)
        def _():
            pivot_rows().start()

        for s in range(1, 4):
            for n, (qx, qy) in enumerate(sources):
                i = at(qx, qy)
                for way in range(2):
                    wait_bytes(panel.at[i, z, h1], r2.at[((s - 1) * 2 + way) * NXY + n])
                    if s < 3:
                        ring(i, s, n, way).start()
                    elif n % 2 == way:
                        ring(i, s, n, way).start()
            cross(-s % NZ, h1)
            cross(s, h1)
        @pl.when(row == 1)
        def _():
            wait_bytes(pc, rp.at[0])

        def other(d):
            wait_bytes(panel.at[:, 0, h0], ro.at[d])
            update0(d)

        load_all.wait()
        wait_bytes(nv, rp.at[1])
        set_weights(pc[...], nv)
        for d in line[:5]:
            update1(d)
        for d in line[:4]:
            other(d)
        for n, (qx, qy) in enumerate(sources):
            i = at(qx, qy)
            wait_bytes(panel.at[i, z, h1], r2.at[(3 * 2 + n % 2) * NXY + n])
        cross(4, h1)
        for d in line[5:]:
            update1(d)
        for d in line[4:]:
            other(d)

    @pl.when(row == 0)
    def _():
        head = mine_ref[0, 0]
        out_ref[0, 0] = jnp.where(jnp.broadcast_to(col, (NB, NB)) == 0, ft[...].T, head)


    @pl.when(core == 0)
    def _():
        wait_sent(v_ref, sp.at[1])

    @pl.when(root)
    def _():
        root_sends(lambda c: c.wait_send())

    @pl.when(core == 0)
    def _():
        second_sends(lambda c: c.wait_send())
    @pl.when(row == 0)
    def _():
        wait_sent(panel.at[0, :, h1], s1.at[1])
        wait_sent(pt.at[h0], s1.at[0])

        @pl.when(core == 1)
        def _():
            wait_sent(pt.at[h0], s1.at[0])

        wait_sent(pc, sp.at[0])

    @pl.when(core == 0)
    def _():
        wait_sent(panel.at[:, :, h0], sd.at[0])
        wait_sent(panel.at[pl.ds(0, 2), pl.ds(0, NZ - 1), h0], sz.at[0])
        wait_sent(panel.at[pl.ds(0, 6), :, h0], s2.at[0])
    @pl.when(core == 1)
    def _():
        wait_sent(panel.at[:, :, h1], sd.at[0])
        wait_sent(panel.at[pl.ds(0, NXY - 1), :, h1], s2.at[0])


def on_device_gather(matrix):
    shape = (NXY, NZ, NB, NB)
    dma = pltpu.SemaphoreType.DMA
    block = pltpu.VMEM((NB, NB), F32)
    return pl.pallas_call(
        step_kernel,
        out_shape=pltpu.VMEM(shape, F32),
        in_specs=[pl.BlockSpec(memory_space=pltpu.HBM)],
        out_specs=pl.BlockSpec(memory_space=pltpu.VMEM),
        scratch_shapes=[pltpu.VMEM(shape, F32)] * 2
        + [block] * 4
        + [pltpu.VMEM((HALF + 8, NB), F32), block, pltpu.VMEM((2 * NB, 2 * NB), BF16)]
        + [dma((2,)), dma((1,)), dma((1,)), dma((1,)), dma((22,)), dma((2,))]
        + [dma((16,)), dma((64,)), dma((8,)), dma((1,)), dma((2,)), dma((2,))],
        compiler_params=pltpu.CompilerParams(
            collective_id=0, has_side_effects=True, vmem_limit_bytes=VMEM_LIMIT
        ),
        name="step",
    )(matrix)


def on_device(matrix):
    local = matrix.reshape(NXY, NZ, NB, NB)
    return on_device_gather(local).reshape(matrix.shape)


def solution(mesh):
    spec = P(None, "row", None, None, "col", None)
    return jax.shard_map(on_device, mesh=mesh, in_specs=(spec,), out_specs=spec, check_vma=False)
```

```python
import functools

import jax
import jax.numpy as jnp
from jax import lax
from jax.experimental import pallas as pl
from jax.experimental.pallas import tpu as pltpu
from jax.sharding import PartitionSpec as P

F32 = jnp.float32
BF16 = jnp.bfloat16
NB = 128
HALF = NB // 2
HA = 56
BLOCKS = 64
NX, NY, NZ = 2, 4, 8
NXY = NX * NY
PIVOTS = 16
VMEM_LIMIT = 56 << 20


def split3(x):
    first = x.astype(BF16)
    rest = x - first.astype(F32)
    second = rest.astype(BF16)
    return first, second, (rest - second.astype(F32)).astype(BF16)


def outer(u, t):
    u1, u2, u3 = split3(u)
    t1, t2, t3 = split3(t)
    left = jnp.concatenate([u1, u1, u2, u2, u1, u3], 0)
    right = jnp.concatenate([t1, t2, t1, t2, t3, t1], 0)
    return lax.dot_general(left, right, (((0,), (0,)), ((), ())), preferred_element_type=F32)


def sweep_block(m_ref, ft_ref, block):
    b = PIVOTS
    groups = b // 8
    o = block * b
    sub = lax.broadcasted_iota(jnp.int32, (8, NB), 0)
    lane = lax.broadcasted_iota(jnp.int32, (8, NB), 1)
    rows = [m_ref[o + 8 * t : o + 8 * t + 8, :] for t in range(groups)]
    work = list(rows)
    cols = [[jnp.broadcast_to(rows[t][:, o + j : o + j + 1], (8, NB)) for t in range(groups)] for j in range(b)]
    factor = [None] * groups
    for j in range(b):
        tj, sj = divmod(j, 8)
        pivot = cols[j][tj][sj : sj + 1, :]
        inverse = 1.0 / pivot
        line = work[tj][sj : sj + 1, :] * lax.rsqrt(pivot)
        factor[tj] = jnp.broadcast_to(line, (8, NB)) if sj == 0 else jnp.where(sub == sj, line, factor[tj])
        work = [
            jnp.where(lane == o + j, jnp.where(sub == sj, 1.0, 0.0) if t == tj else 0.0, work[t])
            for t in range(groups)
        ]
        by = list(cols[j])
        by[tj] = jnp.where(sub == sj, cols[j][tj] - 1.0, cols[j][tj])
        scaled = work[tj][sj : sj + 1, :] * inverse
        work = [work[t] - by[t] * scaled for t in range(groups)]
        for m in range(j + 1, b):
            one = cols[m][tj][sj : sj + 1, :] * inverse
            cols[m] = [cols[m][t] - by[t] * one for t in range(groups)]
    inside = (lane >= o) & (lane < o + b)
    eye = [jnp.where(lane == o + 8 * t + sub, 1.0, 0.0) for t in range(groups)]
    left = jnp.concatenate([rows[t] - eye[t] for t in range(groups)], 0)
    right = jnp.concatenate([jnp.where(inside, eye[t] - work[t], work[t]) for t in range(groups)], 0)
    m_ref[...] = m_ref[...] - outer(left, right)
    for t in range(groups):
        s = slice(o + 8 * t, o + 8 * t + 8)
        m_ref[s, :] = jnp.where(inside, -work[t], work[t])
        ft_ref[s, :] = jnp.where(lane >= o + 8 * t + sub, factor[t], 0.0)


def pack(block):
    sub = lax.broadcasted_iota(jnp.int32, (HALF, NB), 0)
    lane = lax.broadcasted_iota(jnp.int32, (HALF, NB), 1)
    top, bottom = block[:HALF], block[HALF:]
    body = jnp.where(sub > lane, pltpu.roll(bottom, HALF, 1), top)
    diagonal = jnp.sum(jnp.where(lane == sub + HALF, bottom, 0.0), axis=0, keepdims=True)
    return jnp.concatenate([body, jnp.broadcast_to(diagonal, (8, NB))], 0)


def unpack(ref):
    sub = lax.broadcasted_iota(jnp.int32, (HALF, NB), 0)
    lane = lax.broadcasted_iota(jnp.int32, (HALF, NB), 1)
    body = ref[0:HALF, :]
    last = pltpu.roll(jnp.where(sub > lane, body, 0.0), HALF, 1)
    strict = jnp.concatenate([jnp.where(sub < lane, body, 0.0), last], 0)
    diagonal = jnp.broadcast_to(ref[HALF : HALF + 1, :], (HALF, NB))
    diagonal = jnp.concatenate(
        [jnp.where(sub == lane, body, 0.0), jnp.where(lane == sub + HALF, diagonal, 0.0)], 0
    )
    return strict + strict.T + diagonal


def step_kernel(
    mat_ref, out_ref, panel, mine_ref, v_ref, ft, pc, pt, packed, nv, weights,
    s1, sz, s2, sd, sa, sp, r1, r2, ro, ra, rp, lsem
):
    row = lax.axis_index("row")
    col = lax.axis_index("col")
    core = lax.rem(col, 2)
    z = lax.rem(lax.div(col, 2), NZ)
    y = lax.rem(lax.div(col, 2 * NZ), NY)
    x = lax.div(col, 2 * NZ * NY)

    def wrap(v, n):
        return jnp.where(v >= n, v - n, v)

    xs = [x, 1 - x]
    ys = [wrap(y + d, NY) for d in range(NY)]
    zs = [wrap(z + d, NZ) for d in range(NZ)]
    offsets = [(1, 2), (1, 1), (1, 3), (0, 2), (1, 0), (0, 1), (0, 3)]
    line = [0, 1, 7, 2, 6, 3, 5, 4]

    def device(r, bx, by, bz, k):
        return {"row": r, "col": bx * (2 * NZ * NY) + by * (2 * NZ) + bz * 2 + k}

    def at(qx, qy):
        return xs[qx % NX] * NY + ys[qy % NY]

    here = at(0, 0)

    def push(src, dst, send, recv, to):
        return pltpu.make_async_remote_copy(
            src_ref=src, dst_ref=dst, send_sem=send, recv_sem=recv,
            device_id=to, device_id_type=pl.DeviceIdType.MESH,
        )

    sibling = device(row, x, y, z, 1 - core)

    def wait_bytes(ref, sem):
        push(ref, ref, sem, sem, sibling).wait_recv()

    def wait_sent(ref, sem):
        push(ref, ref, sem, sem, sibling).wait_send()

    h0, h1 = pl.ds(0, HA), pl.ds(HA, NB - HA)
    root = (row == 0) & (col == 0)

    load = pltpu.make_async_copy(mat_ref.at[0, 0], pc, lsem.at[0])
    load_all = pltpu.make_async_copy(mat_ref, mine_ref, lsem.at[1])

    @pl.when(row == 0)
    def _():
        load.start()

    load_all.start()

    barrier = pltpu.get_barrier_semaphore()

    def greet(to):
        pl.semaphore_signal(barrier, inc=1, device_id=to, device_id_type=pl.DeviceIdType.MESH)

    greet(sibling)
    greet(device(1 - row, x, y, z, core))
    for d in (1, NZ - 1):
        greet(device(row, x, y, zs[d], core))

    @pl.when(core == 0)
    def _():
        for d in range(2, NZ - 1):
            greet(device(row, x, y, zs[d], 0))
        for qx, qy in offsets:
            greet(device(row, xs[qx], ys[qy], z, 0))

    @pl.when(core == 1)
    def _():
        for qx, qy in offsets:
            greet(device(1 - row, xs[qx], ys[qy], z, 1))

    @pl.when(row == 0)
    def _():
        for qx, qy in offsets:
            greet(device(0, xs[qx], ys[qy], z, 1 - core))

    @pl.when(row != core)
    def _():
        for qx in range(NX):
            greet(device(1 - row, xs[qx], y, z, 1 - core))

    @pl.when(root)
    def _():
        for q in range(1, NXY):
            greet(device(1, q // NY, q % NY, 0, 0))

    @pl.when((row == 1) & (core == 0) & (z == 0) & (here > 0))
    def _():
        greet(device(0, 0, 0, 0, 0))

    heard = 4 + (NZ - 3 + NXY - 1) * (1 - core) + (NXY - 1) * core + (NXY - 1) * (1 - row)
    heard += jnp.where(row != core, NX, 0) + jnp.where(root, NXY - 1, 0)
    heard += jnp.where((row == 1) & (core == 0) & (z == 0) & (here > 0), 1, 0)

    @pl.when(row == 0)
    def _():
        load.wait()
        pt[...] = pc[...].T

        @pl.when(core == 0)
        def _():
            panel[pl.ds(here, 1), pl.ds(z, 1), 0:HA, :] = pt[0:HA, :][None, None]

        @pl.when(col == 0)
        def _():
            packed[...] = pack(pc[...])

    pl.semaphore_wait(barrier, heard)

    def a00_push(i, to):
        return push(packed, packed, sa.at[i], ra.at[0], to)

    def root_sends(act):
        for n, d in enumerate([4, 3, 5, 2, 6, 1, 7]):
            act(a00_push(n, device(0, 0, 0, d, 0)))
        for n, q in enumerate([6, 5, 7, 2, 4, 1, 3, 0]):
            act(a00_push(7 + n, device(1, q // NY, q % NY, 0, 0)))

    def second_sends(act):
        @pl.when((row == 0) & (here == 0))
        def _():
            for n, (qx, qy) in enumerate(offsets):
                act(a00_push(15 + n, device(0, qx, qy, z, 0)))

        @pl.when((row == 1) & (z == 0))
        def _():
            for n, d in enumerate([4, 3, 5, 2, 6, 1, 7]):
                act(a00_push(15 + n, device(1, x, y, d, 0)))

    @pl.when(root)
    def _():
        root_sends(lambda c: c.start())
        second_sends(lambda c: c.start())

    def cross(d, half):
        group = panel.at[:, zs[d], half]
        push(group, group, sd.at[0], ro.at[d], sibling).start()

    def set_weights(rhs, minus_inverse):
        v = jnp.dot(minus_inverse[...], rhs, precision=lax.Precision.HIGHEST, preferred_element_type=F32)
        high = v.astype(BF16)
        low = (v - high.astype(F32)).astype(BF16)
        both = jnp.concatenate([high, low], 1)
        weights[...] = jnp.concatenate([both, both], 0)

    keep = jnp.where(col == 0, 0.0, 1.0)

    def update(d, start, size):
        there = (slice(None), pl.ds(zs[d], 1), slice(start, start + size), slice(None))
        rows = panel[there].reshape(NXY * size, NB)
        high = rows.astype(BF16)
        low = (rows - high.astype(F32)).astype(BF16)
        parts = jnp.dot(jnp.concatenate([high, low], 1), weights[...], preferred_element_type=F32)
        moved = (parts[:, :NB] + parts[:, NB:]).reshape(NXY, 1, size, NB)
        out_ref[there] = mine_ref[there] * keep + moved

    def update0(d):
        update(d, 0, HA)

    def update1(d):
        update(d, HA, NB - HA)

    def along_z(src, q, d):
        return push(src, panel.at[at(q, 0), z, h0], sz.at[0], r1.at[q * NZ + d], device(row, x, y, zs[-d % NZ], 0))

    def first_x(q):
        return push(pt.at[h0], panel.at[here, z, h0], s1.at[0], r1.at[q * NZ], device(core, xs[q], y, z, 0))

    def first_h1(n, qx, qy):
        return push(pt.at[h1], panel.at[here, z, h1], s1.at[1], r1.at[n], device(core, xs[qx], ys[qy], z, 1))

    def pivot_rows():
        return push(pc, pc, sp.at[0], rp.at[0], device(1, x, y, z, core))

    @pl.when(row == 0)
    def _():
        @pl.when(core == 1)
        def _():
            first_x(0).start()

        first_x(1).start()
        first_h1(7, 0, 0).start()
        for n in range(NXY - 1):
            first_h1(n, *offsets[n]).start()

            @pl.when(core == 0)
            def _():
                along_z(pt.at[h0], 0, line[n + 1]).start()

    @pl.when(core == 0)
    def _():
        def along_y(q, d):
            piece = panel.at[at(q, 0), zs[d], h0]
            for qy in (2, 1, 3):
                push(piece, piece, s2.at[0], r2.at[d], device(row, x, ys[qy], z, 0)).start()

        def wait_line(q, d):
            wait_bytes(pt.at[h0], r1.at[q * NZ + d])

        def spread(q):
            for d in line[1:]:
                along_z(panel.at[at(q, 0), z, h0], q, d).start()

        @pl.when(row == 1)
        def _():
            wait_line(0, 0)
            spread(0)

        along_y(0, 0)
        wait_line(1, 0)
        spread(1)
        along_y(1, 0)

        def a00_on():
            @pl.when(((row == 0) & (here == 0) & (col > 0)) | ((row == 1) & (z == 0)))
            def _():
                wait_bytes(packed, ra.at[0])
                second_sends(lambda c: c.start())

        for n, d in enumerate(line[1:]):
            wait_line(0, d)
            along_y(0, d)
            if n == 1:
                a00_on()

        @pl.when(row == 0)
        def _():
            pivot_rows().start()

        for d in line[1:]:
            wait_line(1, d)
            along_y(1, d)

        @pl.when(jnp.logical_not(((row == 0) & (here == 0)) | ((row == 1) & (z == 0))))
        def _():
            wait_bytes(packed, ra.at[0])
        def group(n):
            wait_bytes(panel.at[pl.ds(0, NXY - 2), 0, h0], r2.at[line[n]])
            cross(line[n], h0)

        def other(d):
            wait_bytes(panel.at[:, 0, h1], ro.at[d])
            update1(d)

        v_ref[...] = unpack(packed)
        done = 0
        for n in range(NB // PIVOTS):
            sweep_block(v_ref, ft, n)
            if n >= 3:
                group(done)
                done += 1
        push(v_ref, nv, sp.at[1], rp.at[1], sibling).start()

        @pl.when(row == 1)
        def _():
            wait_bytes(pc, rp.at[0])

        first = jnp.broadcast_to(col, (NB, NB)) == 0
        set_weights(jnp.where(first, -ft[...].T, pc[...]), v_ref)
        load_all.wait()
        for n, (before, theirs) in enumerate([((0, 1), (0,)), ((2, 3), (1, 7)), ((4, 5), (2, 6)), ((6, 7), (3, 5, 4))]):
            for m in before:
                update0(line[m])
            for d in theirs:
                other(d)
            if n < NZ - done:
                group(done + n)

    @pl.when(core == 1)
    def _():
        sources = [(0, 0)] + [(-qx, -qy) for qx, qy in offsets]
        sems = [7, 0, 1, 2, 3, 4, 5, 6]

        def ring(i, s, n, way):
            piece = panel.at[i, zs[-s % NZ] if way == 0 else zs[s], h1]
            to = device(row, x, y, zs[1] if way == 0 else zs[7], 1)
            return push(piece, piece, s2.at[0], r2.at[(s * 2 + way) * NXY + n], to)

        for n, (qx, qy) in enumerate(sources):
            i = at(qx, qy)
            wait_bytes(panel.at[i, z, h1], r1.at[sems[n]])
            for way in range(2):
                ring(i, 0, n, way).start()
        cross(0, h1)

        @pl.when(row == 0)
        def _():
            pivot_rows().start()

        for s in range(1, 4):
            for n, (qx, qy) in enumerate(sources):
                i = at(qx, qy)
                for way in range(2):
                    wait_bytes(panel.at[i, z, h1], r2.at[((s - 1) * 2 + way) * NXY + n])
                    if s < 3:
                        ring(i, s, n, way).start()
                    elif n % 2 == way:
                        ring(i, s, n, way).start()
            cross(-s % NZ, h1)
            cross(s, h1)
        @pl.when(row == 1)
        def _():
            wait_bytes(pc, rp.at[0])

        def other(d):
            wait_bytes(panel.at[:, 0, h0], ro.at[d])
            update0(d)

        load_all.wait()
        wait_bytes(nv, rp.at[1])
        set_weights(pc[...], nv)
        for d in line[:5]:
            update1(d)
        for d in line[:4]:
            other(d)
        for n, (qx, qy) in enumerate(sources):
            i = at(qx, qy)
            wait_bytes(panel.at[i, z, h1], r2.at[(3 * 2 + n % 2) * NXY + n])
            piece = panel.at[i, zs[4], h1]
            push(piece, piece, sd.at[0], ro.at[4], sibling).start()
        for d in line[5:]:
            update1(d)
        for d in line[4:]:
            other(d)

    @pl.when(row == 0)
    def _():
        head = mine_ref[0, 0]
        out_ref[0, 0] = jnp.where(jnp.broadcast_to(col, (NB, NB)) == 0, ft[...].T, head)


    @pl.when(core == 0)
    def _():
        wait_sent(v_ref, sp.at[1])

    @pl.when(root)
    def _():
        root_sends(lambda c: c.wait_send())

    @pl.when(core == 0)
    def _():
        second_sends(lambda c: c.wait_send())
    @pl.when(row == 0)
    def _():
        wait_sent(panel.at[0, :, h1], s1.at[1])
        wait_sent(pt.at[h0], s1.at[0])

        @pl.when(core == 1)
        def _():
            wait_sent(pt.at[h0], s1.at[0])

        wait_sent(pc, sp.at[0])

    @pl.when(core == 0)
    def _():
        wait_sent(panel.at[:, :, h0], sd.at[0])
        wait_sent(panel.at[pl.ds(0, 2), pl.ds(0, NZ - 1), h0], sz.at[0])
        wait_sent(panel.at[pl.ds(0, 6), :, h0], s2.at[0])
    @pl.when(core == 1)
    def _():
        wait_sent(panel.at[:, :, h1], sd.at[0])
        wait_sent(panel.at[pl.ds(0, NXY - 1), :, h1], s2.at[0])


def on_device_gather(matrix):
    shape = (NXY, NZ, NB, NB)
    dma = pltpu.SemaphoreType.DMA
    block = pltpu.VMEM((NB, NB), F32)
    return pl.pallas_call(
        step_kernel,
        out_shape=pltpu.VMEM(shape, F32),
        in_specs=[pl.BlockSpec(memory_space=pltpu.HBM)],
        out_specs=pl.BlockSpec(memory_space=pltpu.VMEM),
        scratch_shapes=[pltpu.VMEM(shape, F32)] * 2
        + [block] * 4
        + [pltpu.VMEM((HALF + 8, NB), F32), block, pltpu.VMEM((2 * NB, 2 * NB), BF16)]
        + [dma((2,)), dma((1,)), dma((1,)), dma((1,)), dma((22,)), dma((2,))]
        + [dma((16,)), dma((64,)), dma((8,)), dma((1,)), dma((2,)), dma((2,))],
        compiler_params=pltpu.CompilerParams(
            collective_id=0, has_side_effects=True, vmem_limit_bytes=VMEM_LIMIT
        ),
        name="step",
    )(matrix)


def on_device(matrix):
    local = matrix.reshape(NXY, NZ, NB, NB)
    return on_device_gather(local).reshape(matrix.shape)


def solution(mesh):
    spec = P(None, "row", None, None, "col", None)
    return jax.shard_map(on_device, mesh=mesh, in_specs=(spec,), out_specs=spec, check_vma=False)
```

```python
import functools

import jax
import jax.numpy as jnp
from jax import lax
from jax.experimental import pallas as pl
from jax.experimental.pallas import tpu as pltpu
from jax.sharding import PartitionSpec as P

F32 = jnp.float32
BF16 = jnp.bfloat16
NB = 128
HALF = NB // 2
HA = 56
BLOCKS = 64
NX, NY, NZ = 2, 4, 8
NXY = NX * NY
PIVOTS = 16
VMEM_LIMIT = 56 << 20


def split3(x):
    first = x.astype(BF16)
    rest = x - first.astype(F32)
    second = rest.astype(BF16)
    return first, second, (rest - second.astype(F32)).astype(BF16)


def outer(u, t):
    u1, u2, u3 = split3(u)
    t1, t2, t3 = split3(t)
    left = jnp.concatenate([u1, u1, u2, u2, u1, u3], 0)
    right = jnp.concatenate([t1, t2, t1, t2, t3, t1], 0)
    return lax.dot_general(left, right, (((0,), (0,)), ((), ())), preferred_element_type=F32)


def sweep_block(m_ref, ft_ref, block):
    b = PIVOTS
    groups = b // 8
    o = block * b
    sub = lax.broadcasted_iota(jnp.int32, (8, NB), 0)
    lane = lax.broadcasted_iota(jnp.int32, (8, NB), 1)
    rows = [m_ref[o + 8 * t : o + 8 * t + 8, :] for t in range(groups)]
    work = list(rows)
    cols = [[jnp.broadcast_to(rows[t][:, o + j : o + j + 1], (8, NB)) for t in range(groups)] for j in range(b)]
    factor = [None] * groups
    for j in range(b):
        tj, sj = divmod(j, 8)
        pivot = cols[j][tj][sj : sj + 1, :]
        inverse = 1.0 / pivot
        line = work[tj][sj : sj + 1, :] * lax.rsqrt(pivot)
        factor[tj] = jnp.broadcast_to(line, (8, NB)) if sj == 0 else jnp.where(sub == sj, line, factor[tj])
        work = [
            jnp.where(lane == o + j, jnp.where(sub == sj, 1.0, 0.0) if t == tj else 0.0, work[t])
            for t in range(groups)
        ]
        by = list(cols[j])
        by[tj] = jnp.where(sub == sj, cols[j][tj] - 1.0, cols[j][tj])
        scaled = work[tj][sj : sj + 1, :] * inverse
        work = [work[t] - by[t] * scaled for t in range(groups)]
        for m in range(j + 1, b):
            one = cols[m][tj][sj : sj + 1, :] * inverse
            cols[m] = [cols[m][t] - by[t] * one for t in range(groups)]
    inside = (lane >= o) & (lane < o + b)
    eye = [jnp.where(lane == o + 8 * t + sub, 1.0, 0.0) for t in range(groups)]
    left = jnp.concatenate([rows[t] - eye[t] for t in range(groups)], 0)
    right = jnp.concatenate([jnp.where(inside, eye[t] - work[t], work[t]) for t in range(groups)], 0)
    m_ref[...] = m_ref[...] - outer(left, right)
    for t in range(groups):
        s = slice(o + 8 * t, o + 8 * t + 8)
        m_ref[s, :] = jnp.where(inside, -work[t], work[t])
        ft_ref[s, :] = jnp.where(lane >= o + 8 * t + sub, factor[t], 0.0)


def pack(block):
    sub = lax.broadcasted_iota(jnp.int32, (HALF, NB), 0)
    lane = lax.broadcasted_iota(jnp.int32, (HALF, NB), 1)
    top, bottom = block[:HALF], block[HALF:]
    body = jnp.where(sub > lane, pltpu.roll(bottom, HALF, 1), top)
    diagonal = jnp.sum(jnp.where(lane == sub + HALF, bottom, 0.0), axis=0, keepdims=True)
    return jnp.concatenate([body, jnp.broadcast_to(diagonal, (8, NB))], 0)


def unpack(ref):
    sub = lax.broadcasted_iota(jnp.int32, (HALF, NB), 0)
    lane = lax.broadcasted_iota(jnp.int32, (HALF, NB), 1)
    body = ref[0:HALF, :]
    last = pltpu.roll(jnp.where(sub > lane, body, 0.0), HALF, 1)
    strict = jnp.concatenate([jnp.where(sub < lane, body, 0.0), last], 0)
    diagonal = jnp.broadcast_to(ref[HALF : HALF + 1, :], (HALF, NB))
    diagonal = jnp.concatenate(
        [jnp.where(sub == lane, body, 0.0), jnp.where(lane == sub + HALF, diagonal, 0.0)], 0
    )
    return strict + strict.T + diagonal


def step_kernel(
    mat_ref, out_ref, panel, mine_ref, v_ref, ft, pc, pt, packed, nv, weights,
    s1, sz, s2, sd, sa, sp, r1, r2, ro, ra, rp, lsem
):
    row = lax.axis_index("row")
    col = lax.axis_index("col")
    core = lax.rem(col, 2)
    z = lax.rem(lax.div(col, 2), NZ)
    y = lax.rem(lax.div(col, 2 * NZ), NY)
    x = lax.div(col, 2 * NZ * NY)

    def wrap(v, n):
        return jnp.where(v >= n, v - n, v)

    xs = [x, 1 - x]
    ys = [wrap(y + d, NY) for d in range(NY)]
    zs = [wrap(z + d, NZ) for d in range(NZ)]
    offsets = [(1, 2), (1, 1), (1, 3), (0, 2), (1, 0), (0, 1), (0, 3)]
    line = [0, 1, 7, 2, 6, 3, 5, 4]

    def device(r, bx, by, bz, k):
        return {"row": r, "col": bx * (2 * NZ * NY) + by * (2 * NZ) + bz * 2 + k}

    def at(qx, qy):
        return xs[qx % NX] * NY + ys[qy % NY]

    here = at(0, 0)

    def push(src, dst, send, recv, to):
        return pltpu.make_async_remote_copy(
            src_ref=src, dst_ref=dst, send_sem=send, recv_sem=recv,
            device_id=to, device_id_type=pl.DeviceIdType.MESH,
        )

    sibling = device(row, x, y, z, 1 - core)

    def wait_bytes(ref, sem):
        push(ref, ref, sem, sem, sibling).wait_recv()

    def wait_sent(ref, sem):
        push(ref, ref, sem, sem, sibling).wait_send()

    h0, h1 = pl.ds(0, HA), pl.ds(HA, NB - HA)
    root = (row == 0) & (col == 0)

    load = pltpu.make_async_copy(mat_ref.at[0, 0], pc, lsem.at[0])
    load_all = pltpu.make_async_copy(mat_ref, mine_ref, lsem.at[1])

    @pl.when(row == 0)
    def _():
        load.start()


    barrier = pltpu.get_barrier_semaphore()

    def greet(to):
        pl.semaphore_signal(barrier, inc=1, device_id=to, device_id_type=pl.DeviceIdType.MESH)

    greet(sibling)
    greet(device(1 - row, x, y, z, core))
    for d in (1, NZ - 1):
        greet(device(row, x, y, zs[d], core))

    @pl.when(core == 0)
    def _():
        for d in range(2, NZ - 1):
            greet(device(row, x, y, zs[d], 0))
        for qx, qy in offsets:
            greet(device(row, xs[qx], ys[qy], z, 0))

    @pl.when(core == 1)
    def _():
        for qx, qy in offsets:
            greet(device(1 - row, xs[qx], ys[qy], z, 1))

    @pl.when(row == 0)
    def _():
        for qx, qy in offsets:
            greet(device(0, xs[qx], ys[qy], z, 1 - core))

    @pl.when(row != core)
    def _():
        for qx in range(NX):
            greet(device(1 - row, xs[qx], y, z, 1 - core))

    @pl.when(root)
    def _():
        for q in range(1, NXY):
            greet(device(1, q // NY, q % NY, 0, 0))

    @pl.when((row == 1) & (core == 0) & (z == 0) & (here > 0))
    def _():
        greet(device(0, 0, 0, 0, 0))

    heard = 4 + (NZ - 3 + NXY - 1) * (1 - core) + (NXY - 1) * core + (NXY - 1) * (1 - row)
    heard += jnp.where(row != core, NX, 0) + jnp.where(root, NXY - 1, 0)
    heard += jnp.where((row == 1) & (core == 0) & (z == 0) & (here > 0), 1, 0)

    @pl.when(row == 0)
    def _():
        load.wait()
        pt[...] = pc[...].T

        @pl.when(core == 0)
        def _():
            panel[pl.ds(here, 1), pl.ds(z, 1), 0:HA, :] = pt[0:HA, :][None, None]

        @pl.when(col == 0)
        def _():
            packed[...] = pack(pc[...])

    pl.semaphore_wait(barrier, heard)

    def a00_push(i, to):
        return push(packed, packed, sa.at[i], ra.at[0], to)

    def root_sends(act):
        for n, d in enumerate([4, 3, 5, 2, 6, 1, 7]):
            act(a00_push(n, device(0, 0, 0, d, 0)))
        for n, q in enumerate([6, 5, 7, 2, 4, 1, 3, 0]):
            act(a00_push(7 + n, device(1, q // NY, q % NY, 0, 0)))

    def second_sends(act):
        @pl.when((row == 0) & (here == 0))
        def _():
            for n, (qx, qy) in enumerate(offsets):
                act(a00_push(15 + n, device(0, qx, qy, z, 0)))

        @pl.when((row == 1) & (z == 0))
        def _():
            for n, d in enumerate([4, 3, 5, 2, 6, 1, 7]):
                act(a00_push(15 + n, device(1, x, y, d, 0)))

    @pl.when(root)
    def _():
        root_sends(lambda c: c.start())
        second_sends(lambda c: c.start())

    def cross(d, half):
        group = panel.at[:, zs[d], half]
        push(group, group, sd.at[0], ro.at[d], sibling).start()

    def set_weights(rhs, minus_inverse):
        v = jnp.dot(minus_inverse[...], rhs, precision=lax.Precision.HIGHEST, preferred_element_type=F32)
        high = v.astype(BF16)
        low = (v - high.astype(F32)).astype(BF16)
        both = jnp.concatenate([high, low], 1)
        weights[...] = jnp.concatenate([both, both], 0)

    keep = jnp.where(col == 0, 0.0, 1.0)

    def update(d, start, size):
        there = (slice(None), pl.ds(zs[d], 1), slice(start, start + size), slice(None))
        rows = panel[there].reshape(NXY * size, NB)
        high = rows.astype(BF16)
        low = (rows - high.astype(F32)).astype(BF16)
        parts = jnp.dot(jnp.concatenate([high, low], 1), weights[...], preferred_element_type=F32)
        moved = (parts[:, :NB] + parts[:, NB:]).reshape(NXY, 1, size, NB)
        out_ref[there] = mine_ref[there] * keep + moved

    def update0(d):
        update(d, 0, HA)

    def update1(d):
        update(d, HA, NB - HA)

    def along_z(src, q, d):
        return push(src, panel.at[at(q, 0), z, h0], sz.at[0], r1.at[q * NZ + d], device(row, x, y, zs[-d % NZ], 0))

    def first_x(q):
        return push(pt.at[h0], panel.at[here, z, h0], s1.at[0], r1.at[q * NZ], device(core, xs[q], y, z, 0))

    def first_h1(n, qx, qy):
        return push(pt.at[h1], panel.at[here, z, h1], s1.at[1], r1.at[n], device(core, xs[qx], ys[qy], z, 1))

    def pivot_rows():
        return push(pc, pc, sp.at[0], rp.at[0], device(1, x, y, z, core))

    @pl.when(row == 0)
    def _():
        @pl.when(core == 1)
        def _():
            first_x(0).start()

        first_x(1).start()
        first_h1(7, 0, 0).start()
        for n in range(NXY - 1):
            first_h1(n, *offsets[n]).start()

            @pl.when(core == 0)
            def _():
                along_z(pt.at[h0], 0, line[n + 1]).start()

    load_all.start()

    @pl.when(core == 0)
    def _():
        def along_y(q, d):
            piece = panel.at[at(q, 0), zs[d], h0]
            for qy in (2, 1, 3):
                push(piece, piece, s2.at[0], r2.at[d], device(row, x, ys[qy], z, 0)).start()

        def wait_line(q, d):
            wait_bytes(pt.at[h0], r1.at[q * NZ + d])

        def spread(q):
            for d in line[1:]:
                along_z(panel.at[at(q, 0), z, h0], q, d).start()

        @pl.when(row == 1)
        def _():
            wait_line(0, 0)
            spread(0)

        along_y(0, 0)
        wait_line(1, 0)
        spread(1)
        along_y(1, 0)

        def a00_on():
            @pl.when(((row == 0) & (here == 0) & (col > 0)) | ((row == 1) & (z == 0)))
            def _():
                wait_bytes(packed, ra.at[0])
                second_sends(lambda c: c.start())

        for n, d in enumerate(line[1:]):
            wait_line(0, d)
            along_y(0, d)
            if n == 1:
                a00_on()

        @pl.when(row == 0)
        def _():
            pivot_rows().start()

        for d in line[1:]:
            wait_line(1, d)
            along_y(1, d)

        @pl.when(jnp.logical_not(((row == 0) & (here == 0)) | ((row == 1) & (z == 0))))
        def _():
            wait_bytes(packed, ra.at[0])
        def group(n):
            wait_bytes(panel.at[pl.ds(0, NXY - 2), 0, h0], r2.at[line[n]])
            cross(line[n], h0)

        def other(d):
            wait_bytes(panel.at[:, 0, h1], ro.at[d])
            update1(d)

        v_ref[...] = unpack(packed)
        done = 0
        for n in range(NB // PIVOTS):
            sweep_block(v_ref, ft, n)
            if n >= 3:
                group(done)
                done += 1
        push(v_ref, nv, sp.at[1], rp.at[1], sibling).start()

        @pl.when(row == 1)
        def _():
            wait_bytes(pc, rp.at[0])

        first = jnp.broadcast_to(col, (NB, NB)) == 0
        set_weights(jnp.where(first, -ft[...].T, pc[...]), v_ref)
        load_all.wait()
        for n, (before, theirs) in enumerate([((0, 1), (0,)), ((2, 3), (1, 7)), ((4, 5), (2, 6)), ((6, 7), (3, 5, 4))]):
            for m in before:
                update0(line[m])
            for d in theirs:
                other(d)
            if n < NZ - done:
                group(done + n)

    @pl.when(core == 1)
    def _():
        sources = [(0, 0)] + [(-qx, -qy) for qx, qy in offsets]
        sems = [7, 0, 1, 2, 3, 4, 5, 6]

        def ring(i, s, n, way):
            piece = panel.at[i, zs[-s % NZ] if way == 0 else zs[s], h1]
            to = device(row, x, y, zs[1] if way == 0 else zs[7], 1)
            return push(piece, piece, s2.at[0], r2.at[(s * 2 + way) * NXY + n], to)

        for n, (qx, qy) in enumerate(sources):
            i = at(qx, qy)
            wait_bytes(panel.at[i, z, h1], r1.at[sems[n]])
            for way in range(2):
                ring(i, 0, n, way).start()
        cross(0, h1)

        @pl.when(row == 0)
        def _():
            pivot_rows().start()

        for s in range(1, 4):
            for n, (qx, qy) in enumerate(sources):
                i = at(qx, qy)
                for way in range(2):
                    wait_bytes(panel.at[i, z, h1], r2.at[((s - 1) * 2 + way) * NXY + n])
                    if s < 3:
                        ring(i, s, n, way).start()
                    elif n % 2 == way:
                        ring(i, s, n, way).start()
            cross(-s % NZ, h1)
            cross(s, h1)
        @pl.when(row == 1)
        def _():
            wait_bytes(pc, rp.at[0])

        def other(d):
            wait_bytes(panel.at[:, 0, h0], ro.at[d])
            update0(d)

        load_all.wait()
        wait_bytes(nv, rp.at[1])
        set_weights(pc[...], nv)
        for d in line[:5]:
            update1(d)
        for d in line[:4]:
            other(d)
        for n, (qx, qy) in enumerate(sources):
            i = at(qx, qy)
            wait_bytes(panel.at[i, z, h1], r2.at[(3 * 2 + n % 2) * NXY + n])
            piece = panel.at[i, zs[4], h1]
            push(piece, piece, sd.at[0], ro.at[4], sibling).start()
        for d in line[5:]:
            update1(d)
        for d in line[4:]:
            other(d)

    @pl.when(row == 0)
    def _():
        head = mine_ref[0, 0]
        out_ref[0, 0] = jnp.where(jnp.broadcast_to(col, (NB, NB)) == 0, ft[...].T, head)


    @pl.when(core == 0)
    def _():
        wait_sent(v_ref, sp.at[1])

    @pl.when(root)
    def _():
        root_sends(lambda c: c.wait_send())

    @pl.when(core == 0)
    def _():
        second_sends(lambda c: c.wait_send())
    @pl.when(row == 0)
    def _():
        wait_sent(panel.at[0, :, h1], s1.at[1])
        wait_sent(pt.at[h0], s1.at[0])

        @pl.when(core == 1)
        def _():
            wait_sent(pt.at[h0], s1.at[0])

        wait_sent(pc, sp.at[0])

    @pl.when(core == 0)
    def _():
        wait_sent(panel.at[:, :, h0], sd.at[0])
        wait_sent(panel.at[pl.ds(0, 2), pl.ds(0, NZ - 1), h0], sz.at[0])
        wait_sent(panel.at[pl.ds(0, 6), :, h0], s2.at[0])
    @pl.when(core == 1)
    def _():
        wait_sent(panel.at[:, :, h1], sd.at[0])
        wait_sent(panel.at[pl.ds(0, NXY - 1), :, h1], s2.at[0])


def on_device_gather(matrix):
    shape = (NXY, NZ, NB, NB)
    dma = pltpu.SemaphoreType.DMA
    block = pltpu.VMEM((NB, NB), F32)
    return pl.pallas_call(
        step_kernel,
        out_shape=pltpu.VMEM(shape, F32),
        in_specs=[pl.BlockSpec(memory_space=pltpu.HBM)],
        out_specs=pl.BlockSpec(memory_space=pltpu.VMEM),
        scratch_shapes=[pltpu.VMEM(shape, F32)] * 2
        + [block] * 4
        + [pltpu.VMEM((HALF + 8, NB), F32), block, pltpu.VMEM((2 * NB, 2 * NB), BF16)]
        + [dma((2,)), dma((1,)), dma((1,)), dma((1,)), dma((22,)), dma((2,))]
        + [dma((16,)), dma((64,)), dma((8,)), dma((1,)), dma((2,)), dma((2,))],
        compiler_params=pltpu.CompilerParams(
            collective_id=0, has_side_effects=True, vmem_limit_bytes=VMEM_LIMIT
        ),
        name="step",
    )(matrix)


def on_device(matrix):
    local = matrix.reshape(NXY, NZ, NB, NB)
    return on_device_gather(local).reshape(matrix.shape)


def solution(mesh):
    spec = P(None, "row", None, None, "col", None)
    return jax.shard_map(on_device, mesh=mesh, in_specs=(spec,), out_specs=spec, check_vma=False)
```
